32 devices in a mesh: context: 16 (over z, y, x), tensor: 2 (over core).
Axes of the slice: x: 2, y: 2, z: 4, core: 2. Of those that a mesh axis runs over, the one named last changes fastest.
Arguments:
- tokens: int32 [8192], P(('context', 'tensor')), may hold values from 0 to 511
- embedding: bfloat16 [512, 1920], replicated, may hold values from -6 to 6
- gain_a: float32 [1920], replicated, may hold values from 0.1 to 1.9
- in_proj_a: bfloat16 [3, 1920, 1920], P(None, 'tensor'), may hold values from -0.125 to 0.125
- short_a: float32 [3, 3, 1920], P(None, None, 'tensor'), may hold values from -4 to 4
- mr_filter: float32 [128, 1920], P(None, 'tensor'), may hold values from -0.5 to 0.5
- mr_skip: float32 [1920], P('tensor'), may hold values from -3 to 3
- out_proj_a: bfloat16 [1920, 1920], P('tensor'), may hold values from -0.125 to 0.125
- gain_b: float32 [1920], replicated, may hold values from 0.1 to 1.9
- in_proj_b: bfloat16 [3, 1920, 1920], P(None, 'tensor'), may hold values from -0.125 to 0.125
- short_b: float32 [3, 3, 1920], P(None, None, 'tensor'), may hold values from -4 to 4
- li_rate: float32 [16, 1920], P(None, 'tensor'), may hold values from 0 to 0.04, as said below
- li_residue: float32 [16, 1920], P(None, 'tensor'), may hold values from -1.5 to 1.5
- li_skip: float32 [1920], P('tensor'), may hold values from -3 to 3
- out_proj_b: bfloat16 [1920, 1920], P('tensor'), may hold values from -0.125 to 0.125
Outputs:
- hidden_out: bfloat16 [8192, 1920], P(('context', 'tensor'))
The draws below stay inside these ranges and needn't reach their ends.
Inputs may be any that keep to these rules, and one draw needn't show every extreme that they name: `li_rate`: every rate lies between 0.05 / 8192 and 1 / 30 per position.
All inputs are finite; a program needn't handle non-finite values.
Results may differ from the reference program's by a relative error of at most 0.014.
Values may be sent and summed in bfloat16 or wider, within the bound.
A program may use at most 192 MiB of HBM per device.

```python
import math
import jax
import jax.numpy as jnp
from jax import lax

D = 1920
VOCAB = 512
MODES = 16
MR_TAPS = 128
SHORT = 3
SEQ = 8192


def draw_li_rate(key, part):
    keys = jax.random.split(key, 3)
    shape = (MODES, D)
    slow_share = 0.5
    slow_pick = jax.random.uniform(keys[0], shape) < slow_share
    slow = jnp.exp(jax.random.uniform(keys[1], shape, minval=math.log(0.05), maxval=math.log(2.0))) / SEQ
    fast = jnp.exp(jax.random.uniform(keys[2], shape, minval=math.log(1.0 / 50.0), maxval=math.log(1.0 / 30.0)))
    return jnp.where(slow_pick, slow, fast).astype(jnp.float32)


def touch_ends(result, key, smallest, high):
    spot = [jax.random.randint(jax.random.fold_in(key, axis), (), 0, length) for axis, length in enumerate(result.shape)]
    main_axis = result.shape.index(max(result.shape))
    beside = spot[:main_axis] + [(spot[main_axis] + 1) % result.shape[main_axis]] + spot[main_axis + 1:]
    return result.at[tuple(spot)].set(smallest).at[tuple(beside)].set(high)


def levels(rng, extent, cuts, smallest, top_value):
    loudness = 1.0
    for dim, blocks in cuts:
        steps = jax.random.uniform(jax.random.fold_in(jax.random.fold_in(rng, 6), dim), (blocks,), jnp.float32, smallest / len(cuts), top_value / len(cuts))
        loudness = loudness * jnp.repeat(jnp.exp(steps), extent[dim] // blocks).reshape((-1,) + (1,) * (len(extent) - 1 - dim))
    return loudness


def normal_values(key, dims, width, most, cuts=(), kind=jnp.bfloat16):
    values = width * jax.random.normal(key, dims, jnp.float32)
    if cuts:
        values = values * levels(key, dims, cuts, -0.22, 0.18)
    return jnp.clip(values, -most, most).astype(kind)


def setup_inputs(seed: int = 0) -> dict:
    key_of = jax.random.split(jax.random.key(seed), 16)
    tokens = touch_ends(jax.random.randint(key_of[0], (SEQ,), 0, VOCAB), jax.random.fold_in(key_of[0], 1), 0, VOCAB - 1).astype(jnp.int32)
    embedding = normal_values(key_of[1], (VOCAB, D), 1.0, 6.0)
    gain_a = jnp.clip(1.0 + 0.18 * jax.random.normal(key_of[2], (D,), jnp.float32), 0.1, 1.9)
    in_proj_a = normal_values(key_of[3], (3, D, D), D ** -0.5, 0.125, ((1, 2),))
    short_a = normal_values(key_of[4], (SHORT, 3, D), 0.6, 4.0, ((2, 2),), jnp.float32)
    mr_filter = normal_values(key_of[5], (MR_TAPS, D), MR_TAPS ** -0.5, 0.5, ((1, 2),), jnp.float32)
    mr_skip = normal_values(key_of[6], (D,), 0.5, 3.0, ((0, 2),), jnp.float32)
    out_proj_a = normal_values(key_of[7], (D, D), D ** -0.5, 0.125, ((0, 2),))
    gain_b = jnp.clip(1.0 + 0.18 * jax.random.normal(key_of[8], (D,), jnp.float32), 0.1, 1.9)
    in_proj_b = normal_values(key_of[9], (3, D, D), D ** -0.5, 0.125, ((1, 2),))
    short_b = normal_values(key_of[10], (SHORT, 3, D), 0.6, 4.0, ((2, 2),), jnp.float32)
    li_rate = draw_li_rate(jax.random.fold_in(key_of[15], 71), 0)
    li_residue = normal_values(key_of[12], (MODES, D), MODES ** -0.5, 1.5, ((1, 2),), jnp.float32)
    li_skip = normal_values(key_of[13], (D,), 0.5, 3.0, ((0, 2),), jnp.float32)
    out_proj_b = normal_values(key_of[14], (D, D), D ** -0.5, 0.125, ((0, 2),))
    return dict(tokens=tokens, embedding=embedding, gain_a=gain_a, in_proj_a=in_proj_a, short_a=short_a, mr_filter=mr_filter, mr_skip=mr_skip, out_proj_a=out_proj_a, gain_b=gain_b, in_proj_b=in_proj_b, short_b=short_b, li_rate=li_rate, li_residue=li_residue, li_skip=li_skip, out_proj_b=out_proj_b)


epsilon = 1e-06
highest = lax.Precision.HIGHEST
block_rows = 128

def normalize(row_data, norm_gain):
    widened = row_data.astype(jnp.float32)
    inverse_rms = lax.rsqrt(lax.optimization_barrier(jnp.mean(widened * widened, axis=1, keepdims=True)) + epsilon)
    return (widened * inverse_rms * norm_gain).astype(jnp.bfloat16)

def featurize(row_data, norm_gain, in_proj, taps):
    features = row_data.shape[1]
    length = row_data.shape[0]
    matrix = in_proj.reshape(-1, features)
    projected = lax.dot_general(normalize(row_data, norm_gain), matrix, (((1,), (1,)), ((), ())), preferred_element_type=jnp.float32).astype(jnp.bfloat16)
    kernel_rows = taps.reshape(taps.shape[0], -1)
    joined = jnp.pad(projected.astype(jnp.float32), ((2, 0), (0, 0)))
    mixture = kernel_rows[0] * joined[2:] + kernel_rows[1] * joined[1:length + 1] + kernel_rows[2] * joined[:length]
    queries = mixture[:, :features]
    gate_prod = (mixture[:, features:2 * features] * mixture[:, 2 * features:]).astype(jnp.bfloat16)
    return (queries, gate_prod)

def medium_conv(gate_prod, kernel):
    length = gate_prod.shape[0]
    padded = jnp.pad(gate_prod.astype(jnp.float32), ((MR_TAPS - 1, 0), (0, 0)))

    def add_tap(tap, running):
        return running + kernel[tap] * lax.dynamic_slice_in_dim(padded, MR_TAPS - 1 - tap, length, 0)
    return lax.fori_loop(0, MR_TAPS, add_tap, jnp.zeros(gate_prod.shape, jnp.float32))

def modal_conv(gate_prod, decay_rate, residue):
    length, features = gate_prod.shape
    ladder = jnp.arange(block_rows).astype(jnp.float32)
    powers = jnp.exp(-decay_rate[None] * ladder[:, None, None])
    modal_gain = residue * jnp.sqrt(-jnp.expm1(-2.0 * decay_rate))
    kernel = jnp.einsum('dmc,mc->dc', powers, modal_gain, precision=highest)
    offsets = jnp.arange(block_rows)[:, None] - jnp.arange(block_rows)[None, :]
    toeplitz = jnp.where((offsets >= 0)[:, :, None], kernel[jnp.clip(offsets, 0, block_rows - 1)], 0.0)
    leading = powers * (jnp.exp(-decay_rate) * modal_gain)[None]
    reversed_powers = powers[::-1]
    step_block = jnp.exp(-decay_rate * block_rows)

    def advance(carry_state, zblock):
        within = jnp.einsum('tsc,sc->tc', toeplitz, zblock, precision=highest)
        carried_in = jnp.einsum('rmc,mc->rc', leading, carry_state, precision=highest)
        new_state = step_block * carry_state + jnp.einsum('smc,sc->mc', reversed_powers, zblock, precision=highest)
        return (new_state, within + carried_in)
    blocks = gate_prod.astype(jnp.float32).reshape(length // block_rows, block_rows, features)
    _, outputs = lax.scan(advance, jnp.zeros(decay_rate.shape, jnp.float32), blocks)
    return outputs.reshape(length, features)

def reference(tokens, embedding, gain_a, in_proj_a, short_a, mr_filter, mr_skip, out_proj_a, gain_b, in_proj_b, short_b, li_rate, li_residue, li_skip, out_proj_b):
    first = embedding[tokens]
    queries, gate_prod = featurize(first, gain_a, in_proj_a, short_a)
    mixture = (queries * (medium_conv(gate_prod, mr_filter) + mr_skip * gate_prod.astype(jnp.float32))).astype(jnp.bfloat16)
    second = (first.astype(jnp.float32) + jnp.dot(mixture, out_proj_a, preferred_element_type=jnp.float32)).astype(jnp.bfloat16)
    queries, gate_prod = featurize(second, gain_b, in_proj_b, short_b)
    mixture = (queries * (modal_conv(gate_prod, li_rate, li_residue) + li_skip * gate_prod.astype(jnp.float32))).astype(jnp.bfloat16)
    return (second.astype(jnp.float32) + jnp.dot(mixture, out_proj_b, preferred_element_type=jnp.float32)).astype(jnp.bfloat16)
```

```python
import functools

import jax
import jax.numpy as jnp
import numpy as np
from jax import lax
from jax.experimental import pallas as pl
from jax.experimental.pallas import tpu as pltpu
from jax.sharding import PartitionSpec as P

EPS = 1e-06
HALO = 160
LEAD = 16
BLOCK = 128
VMEM = 56 * 1024 * 1024
F32 = jnp.float32
BF16 = jnp.bfloat16


def params():
    return pltpu.CompilerParams(vmem_limit_bytes=VMEM)


def split(value):
    high = value.astype(BF16)
    return high, (value - high.astype(F32)).astype(BF16)


def np_split(value):
    high = value.astype(jnp.bfloat16)
    return high, (value - high.astype(np.float64)).astype(jnp.bfloat16)


def transforms():
    bins = np.concatenate([np.arange(0, BLOCK, 2), np.arange(1, BLOCK, 2)])
    angle = np.pi * (2 * bins[:, None] + 1) * np.arange(BLOCK)[None, :] / (2 * BLOCK)
    forward = np.concatenate([np.cos(angle), -np.sin(angle)], 0)
    inverse = forward.T / BLOCK
    fh, fl = np_split(forward)
    ih, il = np_split(inverse)
    return np.concatenate([fh, fl], 1), np.concatenate([ih, il], 1)


def dot(a, b):
    return jnp.dot(a, b, preferred_element_type=F32)


def dot_nt(a, b):
    return lax.dot_general(a, b, (((1,), (1,)), ((), ())), preferred_element_type=F32)


def normalize(rows, gain):
    wide = rows.astype(F32)
    inverse_rms = lax.rsqrt(jnp.mean(wide * wide, axis=1, keepdims=True) + EPS)
    return (wide * inverse_rms * gain).astype(BF16)


def forward_exact(fwd_ref, rows):
    return dot(fwd_ref[...], jnp.concatenate([rows, rows], 0))


def forward_wide(fwd_ref, rows):
    high, low = split(rows)
    return forward_exact(fwd_ref, high) + dot(fwd_ref[:, :BLOCK], low)


def inverse_wide(inv_ref, high_ref, low_ref):
    size = 2 * BLOCK
    return (
        dot(inv_ref[:, :size], high_ref[...])
        + dot(inv_ref[:, size:], high_ref[...])
        + dot(inv_ref[:, :size], low_ref[...])
    )


def onehot(tokens, vocab):
    return (tokens == lax.broadcasted_iota(jnp.int32, (tokens.shape[0], vocab), 1)).astype(BF16)


def short_filter(ref, part, row, count, taps):
    wide = ref[part, pl.ds(row, count + 8), :]
    return (
        taps[0] * wide[8:] + taps[1] * wide[7 : count + 7] + taps[2] * wide[6 : count + 6]
    )


def table_kernel(emb_ref, gain_ref, mat_ref, out_ref, normed):
    rows = emb_ref.shape[0]

    @pl.when(pl.program_id(0) == 0)
    def _():
        @pl.loop(0, rows // 32)
        def _(i):
            at = pl.ds(pl.multiple_of(i * 32, 32), 32)
            normed[at, :] = normalize(emb_ref[at, :], gain_ref[...])

    @pl.loop(0, rows // 256)
    def _(i):
        at = pl.ds(pl.multiple_of(i * 256, 256), 256)
        out_ref[0, at, :] = dot_nt(normed[at, :], mat_ref[0]).astype(BF16)


def make_table(embedding, gain, matrix):
    vocab, width = embedding.shape
    parts, channels, _ = matrix.shape
    return pl.pallas_call(
        table_kernel,
        grid=(parts,),
        in_specs=[
            pl.BlockSpec((vocab, width), lambda i: (0, 0)),
            pl.BlockSpec((1, width), lambda i: (0, 0)),
            pl.BlockSpec((1, channels, width), lambda i: (i, 0, 0)),
        ],
        out_specs=pl.BlockSpec((1, vocab, channels), lambda i: (i, 0, 0)),
        out_shape=jax.ShapeDtypeStruct((parts, vocab, channels), BF16),
        scratch_shapes=[pltpu.VMEM((vocab, width), BF16)],
        compiler_params=params(),
        cost_estimate=pl.CostEstimate(
            flops=2 * vocab * width * channels * parts,
            bytes_accessed=2 * parts * channels * (width + vocab),
            transcendentals=0,
        ),
    )(embedding, gain[None], matrix)


def medium_kernel(
    tok_ref, table_ref, taps_ref, filt_ref, skip_ref, fwd_ref, inv_ref, out_ref,
    proj, gate_f, gate_b, query, spec, freq, zh, zl,
):
    rows = tok_ref.shape[0]
    vocab = table_ref.shape[1]
    channels = table_ref.shape[2]
    length = rows - HALO
    for part in range(3):
        proj[part, 0:8, :] = jnp.zeros((8, channels), F32)
    third = rows // 3
    for i in range(3):
        picked = onehot(tok_ref[i * third : (i + 1) * third, :], vocab)
        for part in range(3):
            proj[part, 8 + i * third : 8 + (i + 1) * third, :] = dot(picked, table_ref[part])

    @pl.loop(0, rows // 32)
    def _(i):
        row = pl.multiple_of(i * 32, 32)
        taps = [[taps_ref[j, pl.ds(part, 1), :] for j in range(3)] for part in range(3)]
        query[pl.ds(row, 32), :] = short_filter(proj, 0, row, 32, taps[0])
        gate = (
            short_filter(proj, 1, row, 32, taps[1]) * short_filter(proj, 2, row, 32, taps[2])
        ).astype(BF16)
        gate_b[pl.ds(row, 32), :] = gate
        gate_f[pl.ds(row, 32), :] = gate.astype(F32)

    filt = filt_ref[...]
    freq[...] = forward_wide(fwd_ref, filt)
    order = lax.broadcasted_iota(jnp.int32, (BLOCK, BLOCK), 0) + lax.broadcasted_iota(
        jnp.int32, (BLOCK, BLOCK), 1
    )
    flip = (order == BLOCK - 1).astype(BF16)
    high, low = split(filt)
    backward = dot(flip, high) + dot(flip, low)
    last = jnp.sum(backward * gate_f[HALO - BLOCK : HALO, :], axis=0, keepdims=True)
    prior = jnp.sum(backward * gate_f[HALO - BLOCK - 1 : HALO - 1, :], axis=0, keepdims=True)
    at = lax.broadcasted_iota(jnp.int32, (LEAD, channels), 0)
    summed = jnp.where(at == LEAD - 1, last, jnp.where(at == LEAD - 2, prior, 0.0))
    edge = slice(HALO - LEAD, HALO)
    out_ref[0:LEAD, :] = jnp.where(
        at >= LEAD - 2, query[edge, :] * (summed + skip_ref[...] * gate_f[edge, :]), 0.0
    ).astype(BF16)

    spec[0] = forward_exact(fwd_ref, gate_b[HALO - BLOCK : HALO, :])
    for b in range(length // BLOCK):
        start = HALO + b * BLOCK
        now, old = (b + 1) % 2, b % 2
        spec[now] = forward_exact(fwd_ref, gate_b[start : start + BLOCK, :])
        for half, sign in ((0, 1.0), (1, -1.0)):

            @pl.loop(0, BLOCK // 64)
            def _(i):
                re = pl.ds(pl.multiple_of(half * (BLOCK // 2) + i * 32, 32), 32)
                im = pl.ds(pl.multiple_of(BLOCK + half * (BLOCK // 2) + i * 32, 32), 32)
                u = spec[now, re, :] - sign * spec[old, im, :]
                v = spec[now, im, :] + sign * spec[old, re, :]
                a, c = freq[re, :], freq[im, :]
                zh[re, :], zl[re, :] = split(u * a - v * c)
                zh[im, :], zl[im, :] = split(u * c + v * a)

        here = slice(start, start + BLOCK)
        conv = inverse_wide(inv_ref, zh, zl)
        out_ref[start - HALO + LEAD : start - HALO + LEAD + BLOCK, :] = (
            query[here, :] * (conv + skip_ref[...] * gate_f[here, :])
        ).astype(BF16)


def medium_mix(tokens, table, taps, filt, skip, fwd, inv):
    rows = tokens.shape[0]
    channels = table.shape[2]
    return pl.pallas_call(
        medium_kernel,
        out_shape=jax.ShapeDtypeStruct((rows - HALO + LEAD, channels), BF16),
        scratch_shapes=[
            pltpu.VMEM((3, rows + 8, channels), F32),
            pltpu.VMEM((rows, channels), F32),
            pltpu.VMEM((rows, channels), BF16),
            pltpu.VMEM((rows, channels), F32),
            pltpu.VMEM((2, 2 * BLOCK, channels), F32),
            pltpu.VMEM((2 * BLOCK, channels), F32),
            pltpu.VMEM((2 * BLOCK, channels), BF16),
            pltpu.VMEM((2 * BLOCK, channels), BF16),
        ],
        compiler_params=params(),
    )(tokens[:, None], table, taps, filt, skip[None], fwd, inv)


def second_kernel(
    tok_ref, emb_ref, mix_ref, out_ref_w, gain_ref, mat_ref, taps_ref, rate_ref,
    second_ref, query_ref, gate_ref, before_ref, closing_ref,
    acc, normed, proj, gate_f,
):
    step = pl.program_id(0)
    rows, width = acc.shape
    vocab = emb_ref.shape[0]
    length = rows - LEAD
    channels = mat_ref.shape[1]
    tile = rows // 3

    @pl.when(step == 0)
    def _():
        @pl.loop(0, 3)
        def _(i):
            at = pl.ds(pl.multiple_of(i * tile, 16), tile)
            picked = onehot(tok_ref[at, :], vocab)
            acc[at, :] = dot(picked, emb_ref[...]) + dot(mix_ref[0, at, :], out_ref_w[0])

    @pl.when(step == 1)
    def _():
        @pl.loop(0, 3)
        def _(i):
            at = pl.ds(pl.multiple_of(i * tile, 16), tile)
            acc[at, :] = acc[at, :] + dot(mix_ref[0, at, :], out_ref_w[0])

        @pl.loop(0, rows // 16)
        def _(i):
            at = pl.ds(pl.multiple_of(i * 16, 16), 16)
            row = acc[at, :].astype(BF16)
            second_ref[at, :] = row
            normed[at, :] = normalize(row, gain_ref[...])

    for stage, part in ((1, 1), (2, 2), (3, 0)):

        @pl.when(step == stage)
        def _():
            @pl.loop(0, 3)
            def _(i):
                at = pl.ds(pl.multiple_of(i * tile, 16), tile)
                proj[part, at, :] = (
                    dot_nt(normed[at, :], mat_ref[0]).astype(BF16).astype(F32)
                )

    @pl.when(step == 2)
    def _():
        taps = [[taps_ref[j, pl.ds(part, 1), :] for j in range(3)] for part in range(3)]

        @pl.loop(0, length // 32)
        def _(i):
            row = pl.multiple_of(i * 32, 32)
            at = pl.multiple_of(row + LEAD - 8, 8)
            gate = (
                short_filter(proj, 1, at, 32, taps[1]) * short_filter(proj, 2, at, 32, taps[2])
            ).astype(BF16)
            gate_ref[pl.ds(row, 32), :] = gate
            gate_f[pl.ds(row, 32), :] = gate.astype(F32)

        decay = jnp.exp(-rate_ref[...])
        state = jnp.zeros(decay.shape, F32)
        for b in range(length // BLOCK):
            before_ref[b] = state

            def advance(i, state):
                tile8 = gate_f[pl.ds(pl.multiple_of(b * BLOCK + i * 8, 8), 8), :]
                for r in range(8):
                    state = state * decay + tile8[r : r + 1, :]
                return state

            state = lax.fori_loop(0, BLOCK // 8, advance, state)
        closing_ref[...] = state.astype(BF16)

    @pl.when(step == 3)
    def _():
        taps = [taps_ref[j, pl.ds(0, 1), :] for j in range(3)]

        @pl.loop(0, length // 32)
        def _(i):
            row = pl.multiple_of(i * 32, 32)
            at = pl.multiple_of(row + LEAD - 8, 8)
            query_ref[pl.ds(row, 32), :] = short_filter(proj, 0, at, 32, taps)


def second_block(tokens, embedding, mixes, weights, gain, matrix, taps, rate):
    _, rows, channels = mixes.shape
    vocab, width = embedding.shape
    length = rows - LEAD
    modes = rate.shape[0]
    whole2 = lambda i: (0, 0)
    whole3 = lambda i: (0, 0, 0)
    return pl.pallas_call(
        second_kernel,
        grid=(4,),
        in_specs=[
            pl.BlockSpec((rows, 1), whole2),
            pl.BlockSpec((vocab, width), whole2),
            pl.BlockSpec((1, rows, channels), lambda i: (jnp.minimum(i, 1), 0, 0)),
            pl.BlockSpec((1, channels, width), lambda i: (jnp.minimum(i, 1), 0, 0)),
            pl.BlockSpec((1, width), whole2),
            pl.BlockSpec(
                (1, channels, width),
                lambda i: (jnp.where(i == 3, 0, jnp.where(i == 2, 2, 1)), 0, 0),
            ),
            pl.BlockSpec(taps.shape, whole3),
            pl.BlockSpec(rate.shape, whole2),
        ],
        out_specs=[
            pl.BlockSpec((rows, width), whole2),
            pl.BlockSpec((length, channels), whole2),
            pl.BlockSpec((length, channels), whole2),
            pl.BlockSpec((length // BLOCK, modes, channels), whole3),
            pl.BlockSpec((modes, channels), whole2),
        ],
        out_shape=[
            jax.ShapeDtypeStruct((rows, width), BF16),
            jax.ShapeDtypeStruct((length, channels), F32),
            jax.ShapeDtypeStruct((length, channels), BF16),
            jax.ShapeDtypeStruct((length // BLOCK, modes, channels), F32),
            jax.ShapeDtypeStruct((modes, channels), BF16),
        ],
        scratch_shapes=[
            pltpu.VMEM((rows, width), F32),
            pltpu.VMEM((rows, width), BF16),
            pltpu.VMEM((3, rows, channels), F32),
            pltpu.VMEM((length, channels), F32),
        ],
        compiler_params=params(),
    )(tokens[:, None], embedding, mixes, weights, gain[None], matrix, taps, rate)


def lanes(channels):
    return [(at, min(128, channels - at)) for at in range(0, channels, 128)]


def modal_rows(rate_ref, coef_ref, groups, lane, width, store):
    modes = rate_ref.shape[0]
    at = lax.broadcasted_iota(jnp.int32, (8, width), 0).astype(F32)
    cols = slice(lane, lane + width)
    values, steps = [], []
    for m in range(modes):
        rate = rate_ref[m : m + 1, cols]
        values.append(coef_ref[m : m + 1, cols] * jnp.exp(-rate * at))
        steps.append(jnp.broadcast_to(jnp.exp(-8.0 * rate), (8, width)))

    def advance(group, values):
        terms = list(values)
        while len(terms) > 1:
            terms = [a + b for a, b in zip(terms[::2], terms[1::2])] + (
                [terms[-1]] if len(terms) % 2 else []
            )
        store(group, terms[0])
        return [v * s for v, s in zip(values, steps)]

    lax.fori_loop(0, groups, advance, values)


def within_kernel(gate_ref, rate_ref, res_ref, skip_ref, fwd_ref, inv_ref, out_ref,
                  coef, taps, freq, spec, zh, zl):
    length, channels = gate_ref.shape
    rate = rate_ref[...]
    doubled = 2.0 * rate
    series = doubled * (1.0 - doubled * (0.5 - doubled * (1.0 / 6.0 - doubled * (1.0 / 24.0 - doubled / 120.0))))
    coef[...] = res_ref[...] * jnp.sqrt(
        jnp.where(doubled < 0.03, series, 1.0 - jnp.exp(-doubled))
    )
    for lane, width in lanes(channels):

        def store(group, rows):
            taps[pl.ds(pl.multiple_of(group * 8, 8), 8), lane : lane + width] = rows

        modal_rows(rate_ref, coef, BLOCK // 8, lane, width, store)
    freq[...] = forward_wide(fwd_ref, taps[...])
    for b in range(length // BLOCK):
        here = slice(b * BLOCK, (b + 1) * BLOCK)
        spec[...] = forward_exact(fwd_ref, gate_ref[here, :])

        @pl.loop(0, BLOCK // 32)
        def _(i):
            re = pl.ds(pl.multiple_of(i * 32, 32), 32)
            im = pl.ds(pl.multiple_of(BLOCK + i * 32, 32), 32)
            u, v = spec[re, :], spec[im, :]
            a, c = freq[re, :], freq[im, :]
            zh[re, :], zl[re, :] = split(u * a - v * c)
            zh[im, :], zl[im, :] = split(u * c + v * a)

        out_ref[here, :] = inverse_wide(inv_ref, zh, zl) + skip_ref[...] * gate_ref[
            here, :
        ].astype(F32)


def within_block(gate, rate, residue, skip, fwd, inv):
    length, channels = gate.shape
    return pl.pallas_call(
        within_kernel,
        out_shape=jax.ShapeDtypeStruct((length, channels), F32),
        scratch_shapes=[
            pltpu.VMEM(rate.shape, F32),
            pltpu.VMEM((BLOCK, channels), F32),
            pltpu.VMEM((2 * BLOCK, channels), F32),
            pltpu.VMEM((2 * BLOCK, channels), F32),
            pltpu.VMEM((2 * BLOCK, channels), BF16),
            pltpu.VMEM((2 * BLOCK, channels), BF16),
        ],
        compiler_params=params(),
        cost_estimate=pl.CostEstimate(
            flops=8_000_000_000, bytes_accessed=4_000_000, transcendentals=0
        ),
    )(gate, rate, residue, skip[None], fwd, inv)


def finish_kernel(pos_ref, seg_ref, rate_ref, res_ref, before_ref, query_ref, within_ref,
                  out_ref, coef):
    length, channels = query_ref.shape
    rate = rate_ref[...]
    shard_step = jnp.exp(-rate * float(length))
    position = pos_ref[0]

    def gather(source, total):
        return jnp.where(
            source < position, total * shard_step + seg_ref[source].astype(F32), total
        )

    incoming = lax.fori_loop(0, seg_ref.shape[0], gather, jnp.zeros(rate.shape, F32))
    doubled = 2.0 * rate
    series = doubled * (1.0 - doubled * (0.5 - doubled * (1.0 / 6.0 - doubled * (1.0 / 24.0 - doubled / 120.0))))
    gain = res_ref[...] * jnp.sqrt(jnp.where(doubled < 0.03, series, 1.0 - jnp.exp(-doubled)))
    for b in range(length // BLOCK):
        coef[b] = (
            gain * jnp.exp(-rate) * (before_ref[b] + jnp.exp(-rate * float(b * BLOCK)) * incoming)
        )
    for b in range(length // BLOCK):
        for lane, width in lanes(channels):
            cols = slice(lane, lane + width)

            def store(group, rows):
                at = pl.ds(pl.multiple_of(b * BLOCK + group * 8, 8), 8)
                out_ref[at, cols] = query_ref[at, cols] * (within_ref[at, cols] + rows)

            modal_rows(rate_ref, coef.at[b], BLOCK // 8, lane, width, store)


def finish_block(position, segments, rate, residue, before, query, within):
    length, channels = query.shape
    return pl.pallas_call(
        finish_kernel,
        in_specs=[pl.BlockSpec(memory_space=pltpu.SMEM)]
        + [pl.BlockSpec(memory_space=pltpu.VMEM)] * 6,
        out_specs=pl.BlockSpec(memory_space=pltpu.VMEM),
        out_shape=jax.ShapeDtypeStruct((length, channels), F32),
        scratch_shapes=[pltpu.VMEM(before.shape, F32)],
        compiler_params=params(),
    )(position, segments, rate, residue, before, query, within)


def on_device(
    tokens, embedding, gain_a, in_proj_a, short_a, mr_filter, mr_skip, out_proj_a,
    gain_b, in_proj_b, short_b, li_rate, li_residue, li_skip, out_proj_b,
):
    fwd, inv = [jnp.asarray(m) for m in transforms()]
    own_rows = tokens.shape[0]
    length = own_rows * lax.axis_size("tensor")
    position = lax.axis_index("context")
    side = lax.axis_index("tensor")
    swap = [(0, 1), (1, 0)]
    all_tokens = lax.all_gather(tokens, ("context", "tensor"), axis=0, tiled=True)
    weights_a = lax.all_gather(out_proj_a, "tensor", axis=0)
    weights_b = lax.ppermute(out_proj_b, "tensor", swap)
    table = make_table(embedding, gain_a, in_proj_a)
    padded = jnp.concatenate([jnp.full((HALO,), -1, jnp.int32), all_tokens])
    near = lax.dynamic_slice_in_dim(padded, position * length, length + HALO, 0)
    mixed = medium_mix(near, table, short_a, mr_filter, mr_skip, fwd, inv)
    mixes = lax.all_gather(mixed, "tensor", axis=0)
    second, query, gate, before, closing = second_block(
        near[HALO - LEAD :], embedding, mixes, weights_a, gain_b, in_proj_b, short_b, li_rate
    )
    segments = lax.all_gather(closing, "context", axis=0)
    within = within_block(gate, li_rate, li_residue, li_skip, fwd, inv)
    mixture = finish_block(
        position[None], segments, li_rate, li_residue, before, query, within
    ).astype(BF16)
    sent = lax.dynamic_slice_in_dim(mixture, (1 - side) * own_rows, own_rows, 0)
    kept = lax.dynamic_slice_in_dim(mixture, side * own_rows, own_rows, 0)
    other = lax.ppermute(sent, "tensor", swap)
    residual = lax.dynamic_slice_in_dim(second, LEAD + side * own_rows, own_rows, 0)
    summed = residual.astype(F32) + dot(kept, out_proj_b)
    return (summed + dot(other, weights_b)).astype(BF16)


def solution(mesh):
    return jax.shard_map(
        on_device,
        mesh=mesh,
        in_specs=(
            P(("context", "tensor")),
            P(),
            P(),
            P(None, "tensor", None),
            P(None, None, "tensor"),
            P(None, "tensor"),
            P("tensor"),
            P("tensor", None),
            P(),
            P(None, "tensor", None),
            P(None, None, "tensor"),
            P(None, "tensor"),
            P(None, "tensor"),
            P("tensor"),
            P("tensor", None),
        ),
        out_specs=P(("context", "tensor"), None),
        check_vma=False,
    )
```

```python
import functools

import jax
import jax.numpy as jnp
import numpy as np
from jax import lax
from jax.experimental import pallas as pl
from jax.experimental.pallas import tpu as pltpu
from jax.sharding import PartitionSpec as P

EPS = 1e-06
HALO = 160
LEAD = 16
BLOCK = 128
VMEM = 56 * 1024 * 1024
F32 = jnp.float32
BF16 = jnp.bfloat16


MESH = pl.DeviceIdType.MESH


def params(collective=None):
    if collective is None:
        return pltpu.CompilerParams(vmem_limit_bytes=VMEM)
    return pltpu.CompilerParams(
        vmem_limit_bytes=VMEM, collective_id=collective, has_side_effects=True
    )


def chunks(total, size=256):
    return [slice(at, min(at + size, total)) for at in range(0, total, size)]


def split(value):
    high = value.astype(BF16)
    return high, (value - high.astype(F32)).astype(BF16)


def np_split(value):
    high = value.astype(jnp.bfloat16)
    return high, (value - high.astype(np.float64)).astype(jnp.bfloat16)


def transforms():
    bins = np.concatenate([np.arange(0, BLOCK, 2), np.arange(1, BLOCK, 2)])
    angle = np.pi * (2 * bins[:, None] + 1) * np.arange(BLOCK)[None, :] / (2 * BLOCK)
    forward = np.concatenate([np.cos(angle), -np.sin(angle)], 0)
    inverse = forward.T / BLOCK
    fh, fl = np_split(forward)
    ih, il = np_split(inverse)
    return np.concatenate([fh, fl], 1), np.concatenate([ih, il], 1)


def dot(a, b):
    return jnp.dot(a, b, preferred_element_type=F32)


def dot_nt(a, b):
    return lax.dot_general(a, b, (((1,), (1,)), ((), ())), preferred_element_type=F32)


def normalize(rows, gain):
    wide = rows.astype(F32)
    inverse_rms = lax.rsqrt(jnp.mean(wide * wide, axis=1, keepdims=True) + EPS)
    return (wide * inverse_rms * gain).astype(BF16)


def forward_exact(fwd_ref, rows):
    return dot(fwd_ref[...], jnp.concatenate([rows, rows], 0))


def forward_wide(fwd_ref, rows):
    high, low = split(rows)
    return forward_exact(fwd_ref, high) + dot(fwd_ref[:, :BLOCK], low)


def inverse_wide(inv_ref, high_ref, low_ref):
    size = 2 * BLOCK
    return (
        dot(inv_ref[:, :size], high_ref[...])
        + dot(inv_ref[:, size:], high_ref[...])
        + dot(inv_ref[:, :size], low_ref[...])
    )


def onehot(tokens, vocab):
    return (tokens == lax.broadcasted_iota(jnp.int32, (tokens.shape[0], vocab), 1)).astype(BF16)


def short_filter(ref, part, row, count, taps):
    wide = ref[part, pl.ds(row, count + 8), :]
    return (
        taps[0] * wide[8:] + taps[1] * wide[7 : count + 7] + taps[2] * wide[6 : count + 6]
    )


def table_kernel(emb_ref, gain_ref, mat_ref, out_ref, normed):
    rows = emb_ref.shape[0]

    @pl.when(pl.program_id(0) == 0)
    def _():
        @pl.loop(0, rows // 32)
        def _(i):
            at = pl.ds(pl.multiple_of(i * 32, 32), 32)
            normed[at, :] = normalize(emb_ref[at, :], gain_ref[...])

    for cols in chunks(mat_ref.shape[1]):
        out_ref[0, :, cols] = dot_nt(normed[...], mat_ref[0, cols, :]).astype(BF16)


def make_table(embedding, gain, matrix):
    vocab, width = embedding.shape
    parts, channels, _ = matrix.shape
    return pl.pallas_call(
        table_kernel,
        grid=(parts,),
        in_specs=[
            pl.BlockSpec((vocab, width), lambda i: (0, 0)),
            pl.BlockSpec((1, width), lambda i: (0, 0)),
            pl.BlockSpec((1, channels, width), lambda i: (i, 0, 0)),
        ],
        out_specs=pl.BlockSpec((1, vocab, channels), lambda i: (i, 0, 0)),
        out_shape=jax.ShapeDtypeStruct((parts, vocab, channels), BF16),
        scratch_shapes=[pltpu.VMEM((vocab, width), BF16)],
        compiler_params=params(),
        cost_estimate=pl.CostEstimate(
            flops=2 * vocab * width * channels * parts,
            bytes_accessed=2 * parts * channels * (width + vocab),
            transcendentals=0,
        ),
    )(embedding, gain[None], matrix)


def medium_kernel(
    tok_ref, table_ref, taps_ref, filt_ref, skip_ref, fwd_ref, inv_ref, out_ref, peer_ref,
    proj, gate_f, gate_b, query, spec, freq, zh, zl, inbox, send_sem, recv_sem,
):
    peer = 1 - lax.axis_index("tensor")
    barrier = pltpu.get_barrier_semaphore()
    pl.semaphore_signal(barrier, inc=1, device_id={"tensor": peer}, device_id_type=MESH)
    rows = tok_ref.shape[0]
    vocab = table_ref.shape[1]
    channels = table_ref.shape[2]
    length = rows - HALO
    for part in range(3):
        proj[part, 0:8, :] = jnp.zeros((8, channels), F32)
    third = rows // 3
    for i in range(3):
        picked = onehot(tok_ref[i * third : (i + 1) * third, :], vocab)
        for part in range(3):
            proj[part, 8 + i * third : 8 + (i + 1) * third, :] = dot(picked, table_ref[part])

    @pl.loop(0, rows // 32)
    def _(i):
        row = pl.multiple_of(i * 32, 32)
        taps = [[taps_ref[j, pl.ds(part, 1), :] for j in range(3)] for part in range(3)]
        query[pl.ds(row, 32), :] = short_filter(proj, 0, row, 32, taps[0])
        gate = (
            short_filter(proj, 1, row, 32, taps[1]) * short_filter(proj, 2, row, 32, taps[2])
        ).astype(BF16)
        gate_b[pl.ds(row, 32), :] = gate
        gate_f[pl.ds(row, 32), :] = gate.astype(F32)

    filt = filt_ref[...]
    freq[...] = forward_wide(fwd_ref, filt)
    order = lax.broadcasted_iota(jnp.int32, (BLOCK, BLOCK), 0) + lax.broadcasted_iota(
        jnp.int32, (BLOCK, BLOCK), 1
    )
    flip = (order == BLOCK - 1).astype(BF16)
    high, low = split(filt)
    backward = dot(flip, high) + dot(flip, low)
    last = jnp.sum(backward * gate_f[HALO - BLOCK : HALO, :], axis=0, keepdims=True)
    prior = jnp.sum(backward * gate_f[HALO - BLOCK - 1 : HALO - 1, :], axis=0, keepdims=True)
    at = lax.broadcasted_iota(jnp.int32, (LEAD, channels), 0)
    summed = jnp.where(at == LEAD - 1, last, jnp.where(at == LEAD - 2, prior, 0.0))
    edge = slice(HALO - LEAD, HALO)
    out_ref[0:LEAD, :] = jnp.where(
        at >= LEAD - 2, query[edge, :] * (summed + skip_ref[...] * gate_f[edge, :]), 0.0
    ).astype(BF16)

    pl.semaphore_wait(barrier, 1)
    copies = []
    spec[0] = forward_exact(fwd_ref, gate_b[HALO - BLOCK : HALO, :])
    for b in range(length // BLOCK):
        start = HALO + b * BLOCK
        now, old = (b + 1) % 2, b % 2
        spec[now] = forward_exact(fwd_ref, gate_b[start : start + BLOCK, :])
        for half, sign in ((0, 1.0), (1, -1.0)):

            @pl.loop(0, BLOCK // 64)
            def _(i):
                re = pl.ds(pl.multiple_of(half * (BLOCK // 2) + i * 32, 32), 32)
                im = pl.ds(pl.multiple_of(BLOCK + half * (BLOCK // 2) + i * 32, 32), 32)
                u = spec[now, re, :] - sign * spec[old, im, :]
                v = spec[now, im, :] + sign * spec[old, re, :]
                a, c = freq[re, :], freq[im, :]
                zh[re, :], zl[re, :] = split(u * a - v * c)
                zh[im, :], zl[im, :] = split(u * c + v * a)

        here = slice(start, start + BLOCK)
        conv = inverse_wide(inv_ref, zh, zl)
        out_ref[start - HALO + LEAD : start - HALO + LEAD + BLOCK, :] = (
            query[here, :] * (conv + skip_ref[...] * gate_f[here, :])
        ).astype(BF16)
        first = 0 if b == 0 else LEAD + b * BLOCK
        part = pl.ds(first, LEAD + (b + 1) * BLOCK - first)
        copy = pltpu.make_async_remote_copy(
            src_ref=out_ref.at[part],
            dst_ref=inbox.at[part],
            send_sem=send_sem.at[b],
            recv_sem=recv_sem.at[b],
            device_id={"tensor": peer},
            device_id_type=MESH,
        )
        copy.start()
        copies.append(copy)
    for copy in copies:
        copy.wait()
    peer_ref[...] = inbox[...]


def medium_mix(tokens, table, taps, filt, skip, fwd, inv):
    rows = tokens.shape[0]
    channels = table.shape[2]
    return pl.pallas_call(
        medium_kernel,
        out_shape=[jax.ShapeDtypeStruct((rows - HALO + LEAD, channels), BF16)] * 2,
        scratch_shapes=[
            pltpu.VMEM((3, rows + 8, channels), F32),
            pltpu.VMEM((rows, channels), F32),
            pltpu.VMEM((rows, channels), BF16),
            pltpu.VMEM((rows, channels), F32),
            pltpu.VMEM((2, 2 * BLOCK, channels), F32),
            pltpu.VMEM((2 * BLOCK, channels), F32),
            pltpu.VMEM((2 * BLOCK, channels), BF16),
            pltpu.VMEM((2 * BLOCK, channels), BF16),
            pltpu.VMEM((rows - HALO + LEAD, channels), BF16),
            pltpu.SemaphoreType.DMA(((rows - HALO) // BLOCK,)),
            pltpu.SemaphoreType.DMA(((rows - HALO) // BLOCK,)),
        ],
        compiler_params=params(0),
    )(tokens[:, None], table, taps, filt, skip[None], fwd, inv)


def second_kernel(
    tok_ref, emb_ref, mix_ref, peer_ref, own_w, peer_w, gain_ref, mat_ref, taps_ref, rate_ref,
    second_ref, query_ref, gate_ref, before_ref, closing_ref,
    acc, normed, proj, gate_f, weight, weight_sem,
):
    step = pl.program_id(0)
    rows, width = acc.shape
    vocab = emb_ref.shape[0]
    length = rows - LEAD
    channels = mat_ref.shape[1]
    fetch = pltpu.make_async_copy(peer_w, weight, weight_sem)

    @pl.when(step == 0)
    def _():
        fetch.start()
        picked = onehot(tok_ref[...], vocab)
        for cols in chunks(width, 384):
            acc[:, cols] = dot(picked, emb_ref[:, cols]) + dot(mix_ref[...], own_w[:, cols])

    @pl.when(step == 1)
    def _():
        fetch.wait()
        for cols in chunks(width, 384):
            acc[:, cols] = acc[:, cols] + dot(peer_ref[...], weight[:, cols])

        @pl.loop(0, rows // 16)
        def _(i):
            at = pl.ds(pl.multiple_of(i * 16, 16), 16)
            row = acc[at, :].astype(BF16)
            second_ref[at, :] = row
            normed[at, :] = normalize(row, gain_ref[...])

    for stage, part in ((1, 1), (2, 2), (3, 0)):

        @pl.when(step == stage)
        def _():
            for cols in chunks(channels):
                proj[part, :, cols] = (
                    dot_nt(normed[...], mat_ref[0, cols, :]).astype(BF16).astype(F32)
                )

    @pl.when(step == 2)
    def _():
        taps = [[taps_ref[j, pl.ds(part, 1), :] for j in range(3)] for part in range(3)]

        @pl.loop(0, length // 32)
        def _(i):
            row = pl.multiple_of(i * 32, 32)
            at = pl.multiple_of(row + LEAD - 8, 8)
            gate = (
                short_filter(proj, 1, at, 32, taps[1]) * short_filter(proj, 2, at, 32, taps[2])
            ).astype(BF16)
            gate_ref[pl.ds(row, 32), :] = gate
            gate_f[pl.ds(row, 32), :] = gate.astype(F32)

        decay = jnp.exp(-rate_ref[...])
        state = jnp.zeros(decay.shape, F32)
        for b in range(length // BLOCK):
            before_ref[b] = state

            def advance(i, state):
                tile8 = gate_f[pl.ds(pl.multiple_of(b * BLOCK + i * 8, 8), 8), :]
                for r in range(8):
                    state = state * decay + tile8[r : r + 1, :]
                return state

            state = lax.fori_loop(0, BLOCK // 8, advance, state)
        closing_ref[...] = state.astype(BF16)

    @pl.when(step == 3)
    def _():
        taps = [taps_ref[j, pl.ds(0, 1), :] for j in range(3)]

        @pl.loop(0, length // 32)
        def _(i):
            row = pl.multiple_of(i * 32, 32)
            at = pl.multiple_of(row + LEAD - 8, 8)
            query_ref[pl.ds(row, 32), :] = short_filter(proj, 0, at, 32, taps)


def second_block(tokens, embedding, mix, peer_mix, weights, peer_weights, gain, matrix, taps, rate):
    rows, channels = mix.shape
    vocab, width = embedding.shape
    length = rows - LEAD
    modes = rate.shape[0]
    whole2 = lambda i: (0, 0)
    whole3 = lambda i: (0, 0, 0)
    return pl.pallas_call(
        second_kernel,
        grid=(4,),
        in_specs=[
            pl.BlockSpec((rows, 1), whole2),
            pl.BlockSpec((vocab, width), whole2),
            pl.BlockSpec((rows, channels), whole2),
            pl.BlockSpec((rows, channels), whole2),
            pl.BlockSpec((channels, width), whole2),
            pl.BlockSpec(memory_space=pl.ANY),
            pl.BlockSpec((1, width), whole2),
            pl.BlockSpec(
                (1, channels, width),
                lambda i: (jnp.where(i == 3, 0, jnp.where(i == 2, 2, 1)), 0, 0),
            ),
            pl.BlockSpec(taps.shape, whole3),
            pl.BlockSpec(rate.shape, whole2),
        ],
        out_specs=[
            pl.BlockSpec((rows, width), whole2),
            pl.BlockSpec((length, channels), whole2),
            pl.BlockSpec((length, channels), whole2),
            pl.BlockSpec((length // BLOCK, modes, channels), whole3),
            pl.BlockSpec((modes, channels), whole2),
        ],
        out_shape=[
            jax.ShapeDtypeStruct((rows, width), BF16),
            jax.ShapeDtypeStruct((length, channels), F32),
            jax.ShapeDtypeStruct((length, channels), BF16),
            jax.ShapeDtypeStruct((length // BLOCK, modes, channels), F32),
            jax.ShapeDtypeStruct((modes, channels), BF16),
        ],
        scratch_shapes=[
            pltpu.VMEM((rows, width), F32),
            pltpu.VMEM((rows, width), BF16),
            pltpu.VMEM((3, rows, channels), F32),
            pltpu.VMEM((length, channels), F32),
            pltpu.VMEM((channels, width), BF16),
            pltpu.SemaphoreType.DMA,
        ],
        compiler_params=params(),
    )(tokens[:, None], embedding, mix, peer_mix, weights, peer_weights, gain[None], matrix, taps, rate)


def lanes(channels):
    return [(at, min(128, channels - at)) for at in range(0, channels, 128)]


def modal_rows(rate_ref, coef_ref, groups, lane, width, store):
    modes = rate_ref.shape[0]
    at = lax.broadcasted_iota(jnp.int32, (8, width), 0).astype(F32)
    cols = slice(lane, lane + width)
    values, steps = [], []
    for m in range(modes):
        rate = rate_ref[m : m + 1, cols]
        values.append(coef_ref[m : m + 1, cols] * jnp.exp(-rate * at))
        steps.append(jnp.broadcast_to(jnp.exp(-8.0 * rate), (8, width)))

    def advance(group, values):
        terms = list(values)
        while len(terms) > 1:
            terms = [a + b for a, b in zip(terms[::2], terms[1::2])] + (
                [terms[-1]] if len(terms) % 2 else []
            )
        store(group, terms[0])
        return [v * s for v, s in zip(values, steps)]

    lax.fori_loop(0, groups, advance, values)


def tail_kernel(
    size, closing_ref, gate_ref, rate_ref, res_ref, skip_ref, fwd_ref, inv_ref, before_ref,
    query_ref, out_ref, segments, enter, gain, taps, freq, spec, zh, zl, total,
    send_sem, recv_sem,
):
    me = lax.axis_index("context")
    barrier = pltpu.get_barrier_semaphore()
    for hop in range(1, size):
        pl.semaphore_signal(
            barrier, inc=1, device_id={"context": lax.rem(me + hop, size)}, device_id_type=MESH
        )
    segments[me] = closing_ref[...]
    length, channels = gate_ref.shape
    rate = rate_ref[...]
    doubled = 2.0 * rate
    series = doubled * (
        1.0
        - doubled * (0.5 - doubled * (1.0 / 6.0 - doubled * (1.0 / 24.0 - doubled / 120.0)))
    )
    gain[...] = res_ref[...] * jnp.sqrt(
        jnp.where(doubled < 0.03, series, 1.0 - jnp.exp(-doubled))
    )
    pl.semaphore_wait(barrier, size - 1)
    copies = []
    for hop in range(1, size):
        copy = pltpu.make_async_remote_copy(
            src_ref=closing_ref,
            dst_ref=segments.at[me],
            send_sem=send_sem.at[hop],
            recv_sem=recv_sem.at[hop],
            device_id={"context": lax.rem(me + hop, size)},
            device_id_type=MESH,
        )
        copy.start()
        copies.append(copy)
    for lane, width in lanes(channels):

        def store(group, rows):
            taps[pl.ds(pl.multiple_of(group * 8, 8), 8), lane : lane + width] = rows

        modal_rows(rate_ref, gain, BLOCK // 8, lane, width, store)
    freq[...] = forward_wide(fwd_ref, taps[...])
    for b in range(length // BLOCK):
        here = slice(b * BLOCK, (b + 1) * BLOCK)
        spec[...] = forward_exact(fwd_ref, gate_ref[here, :])

        @pl.loop(0, BLOCK // 32)
        def _(i):
            re = pl.ds(pl.multiple_of(i * 32, 32), 32)
            im = pl.ds(pl.multiple_of(BLOCK + i * 32, 32), 32)
            u, v = spec[re, :], spec[im, :]
            a, c = freq[re, :], freq[im, :]
            zh[re, :], zl[re, :] = split(u * a - v * c)
            zh[im, :], zl[im, :] = split(u * c + v * a)

        total[here, :] = inverse_wide(inv_ref, zh, zl) + skip_ref[...] * gate_ref[
            here, :
        ].astype(F32)

    for copy in copies:
        copy.wait()
    shard_step = jnp.exp(-rate * float(length))
    incoming = jnp.zeros(rate.shape, F32)
    for source in range(size):
        incoming = jnp.where(
            source < me, incoming * shard_step + segments[source].astype(F32), incoming
        )
    for b in range(length // BLOCK):
        enter[b] = (
            gain[...]
            * jnp.exp(-rate)
            * (before_ref[b] + jnp.exp(-rate * float(b * BLOCK)) * incoming)
        )
    for b in range(length // BLOCK):
        for lane, width in lanes(channels):
            cols = slice(lane, lane + width)

            def store(group, rows):
                at = pl.ds(pl.multiple_of(b * BLOCK + group * 8, 8), 8)
                total[at, cols] = query_ref[at, cols] * (total[at, cols] + rows)

            modal_rows(rate_ref, enter.at[b], BLOCK // 8, lane, width, store)
        here = slice(b * BLOCK, (b + 1) * BLOCK)
        out_ref[here, :] = total[here, :].astype(BF16)


def tail_block(size, closing, gate, rate, residue, skip, fwd, inv, before, query):
    length, channels = gate.shape
    return pl.pallas_call(
        functools.partial(tail_kernel, size),
        in_specs=[pl.BlockSpec(memory_space=pltpu.VMEM)] * 9,
        out_specs=pl.BlockSpec(memory_space=pltpu.VMEM),
        out_shape=jax.ShapeDtypeStruct((length, channels), BF16),
        scratch_shapes=[
            pltpu.VMEM((size,) + closing.shape, BF16),
            pltpu.VMEM(before.shape, F32),
            pltpu.VMEM(rate.shape, F32),
            pltpu.VMEM((BLOCK, channels), F32),
            pltpu.VMEM((2 * BLOCK, channels), F32),
            pltpu.VMEM((2 * BLOCK, channels), F32),
            pltpu.VMEM((2 * BLOCK, channels), BF16),
            pltpu.VMEM((2 * BLOCK, channels), BF16),
            pltpu.VMEM((length, channels), F32),
            pltpu.SemaphoreType.DMA((size,)),
            pltpu.SemaphoreType.DMA((size,)),
        ],
        compiler_params=params(1),
    )(closing, gate, rate, residue, skip[None], fwd, inv, before, query)


def on_device(
    tokens, embedding, gain_a, in_proj_a, short_a, mr_filter, mr_skip, out_proj_a,
    gain_b, in_proj_b, short_b, li_rate, li_residue, li_skip, out_proj_b,
):
    fwd, inv = [jnp.asarray(m) for m in transforms()]
    own_rows = tokens.shape[0]
    length = own_rows * lax.axis_size("tensor")
    position = lax.axis_index("context")
    side = lax.axis_index("tensor")
    swap = [(0, 1), (1, 0)]
    size = lax.axis_size("context")
    both = ("context", "tensor")
    other_tokens = lax.ppermute(tokens, "tensor", swap)
    edge = tokens[own_rows - HALO :]
    halo = sum(
        lax.ppermute(edge, both, [(2 * c + 1, 2 * c + 2 + t) for c in range(size - 1)])
        for t in range(2)
    )
    weights_a = lax.ppermute(out_proj_a, "tensor", swap)
    weights_b = lax.ppermute(out_proj_b, "tensor", swap)
    table = make_table(embedding, gain_a, in_proj_a)
    near = jnp.concatenate(
        [
            jnp.where(position == 0, -1, halo),
            jnp.where(side == 0, tokens, other_tokens),
            jnp.where(side == 0, other_tokens, tokens),
        ]
    )
    mixed, peer_mixed = medium_mix(near, table, short_a, mr_filter, mr_skip, fwd, inv)
    second, query, gate, before, closing = second_block(
        near[HALO - LEAD :], embedding, mixed, peer_mixed, out_proj_a, weights_a, gain_b,
        in_proj_b, short_b, li_rate,
    )
    mixture = tail_block(
        size, closing, gate, li_rate, li_residue, li_skip, fwd, inv, before, query
    )
    sent = lax.dynamic_slice_in_dim(mixture, (1 - side) * own_rows, own_rows, 0)
    kept = lax.dynamic_slice_in_dim(mixture, side * own_rows, own_rows, 0)
    other = lax.ppermute(sent, "tensor", swap)
    residual = lax.dynamic_slice_in_dim(second, LEAD + side * own_rows, own_rows, 0)
    summed = residual.astype(F32) + dot(kept, out_proj_b)
    return (summed + dot(other, weights_b)).astype(BF16)


def solution(mesh):
    return jax.shard_map(
        on_device,
        mesh=mesh,
        in_specs=(
            P(("context", "tensor")),
            P(),
            P(),
            P(None, "tensor", None),
            P(None, None, "tensor"),
            P(None, "tensor"),
            P("tensor"),
            P("tensor", None),
            P(),
            P(None, "tensor", None),
            P(None, None, "tensor"),
            P(None, "tensor"),
            P(None, "tensor"),
            P("tensor"),
            P("tensor", None),
        ),
        out_specs=P(("context", "tensor"), None),
        check_vma=False,
    )
```

```python
import functools

import jax
import jax.numpy as jnp
import numpy as np
from jax import lax
from jax.experimental import pallas as pl
from jax.experimental.pallas import tpu as pltpu
from jax.sharding import PartitionSpec as P

EPS = 1e-06
HALO = 160
LEAD = 16
BLOCK = 128
VMEM = 56 * 1024 * 1024
F32 = jnp.float32
BF16 = jnp.bfloat16


MESH = pl.DeviceIdType.MESH


def params(collective=None):
    if collective is None:
        return pltpu.CompilerParams(vmem_limit_bytes=VMEM)
    return pltpu.CompilerParams(
        vmem_limit_bytes=VMEM, collective_id=collective, has_side_effects=True
    )


def chunks(total, size=256):
    return [slice(at, min(at + size, total)) for at in range(0, total, size)]


def split(value):
    high = value.astype(BF16)
    return high, (value - high.astype(F32)).astype(BF16)


def np_split(value):
    high = value.astype(jnp.bfloat16)
    return high, (value - high.astype(np.float64)).astype(jnp.bfloat16)


def transforms():
    bins = np.concatenate([np.arange(0, BLOCK, 2), np.arange(1, BLOCK, 2)])
    angle = np.pi * (2 * bins[:, None] + 1) * np.arange(BLOCK)[None, :] / (2 * BLOCK)
    forward = np.concatenate([np.cos(angle), -np.sin(angle)], 0)
    inverse = forward.T / BLOCK
    fh, fl = np_split(forward)
    ih, il = np_split(inverse)
    return np.concatenate([fh, fl], 1), np.concatenate([ih, il], 1)


def dot(a, b):
    return jnp.dot(a, b, preferred_element_type=F32)


def dot_nt(a, b):
    return lax.dot_general(a, b, (((1,), (1,)), ((), ())), preferred_element_type=F32)


def normalize(rows, gain):
    wide = rows.astype(F32)
    inverse_rms = lax.rsqrt(jnp.mean(wide * wide, axis=1, keepdims=True) + EPS)
    return (wide * inverse_rms * gain).astype(BF16)


def forward_exact(fwd_ref, rows):
    return dot(fwd_ref[...], jnp.concatenate([rows, rows], 0))


def forward_wide(fwd_ref, rows):
    high, low = split(rows)
    return forward_exact(fwd_ref, high) + dot(fwd_ref[:, :BLOCK], low)


def inverse_wide(inv_ref, high_ref, low_ref):
    size = 2 * BLOCK
    return (
        dot(inv_ref[:, :size], high_ref[...])
        + dot(inv_ref[:, size:], high_ref[...])
        + dot(inv_ref[:, :size], low_ref[...])
    )


def onehot(tokens, vocab):
    return (tokens == lax.broadcasted_iota(jnp.int32, (tokens.shape[0], vocab), 1)).astype(BF16)


def short_filter(ref, part, row, count, taps):
    wide = ref[part, pl.ds(row, count + 8), :]
    return (
        taps[0] * wide[8:] + taps[1] * wide[7 : count + 7] + taps[2] * wide[6 : count + 6]
    )


def table_kernel(emb_ref, gain_ref, mat_ref, out_ref, normed):
    rows = emb_ref.shape[0]

    @pl.when(pl.program_id(0) == 0)
    def _():
        @pl.loop(0, rows // 32)
        def _(i):
            at = pl.ds(pl.multiple_of(i * 32, 32), 32)
            normed[at, :] = normalize(emb_ref[at, :], gain_ref[...])

    for cols in chunks(mat_ref.shape[1]):
        out_ref[0, :, cols] = dot_nt(normed[...], mat_ref[0, cols, :]).astype(BF16)


def make_table(embedding, gain, matrix):
    vocab, width = embedding.shape
    parts, channels, _ = matrix.shape
    return pl.pallas_call(
        table_kernel,
        grid=(parts,),
        in_specs=[
            pl.BlockSpec((vocab, width), lambda i: (0, 0)),
            pl.BlockSpec((1, width), lambda i: (0, 0)),
            pl.BlockSpec((1, channels, width), lambda i: (i, 0, 0)),
        ],
        out_specs=pl.BlockSpec((1, vocab, channels), lambda i: (i, 0, 0)),
        out_shape=jax.ShapeDtypeStruct((parts, vocab, channels), BF16),
        scratch_shapes=[pltpu.VMEM((vocab, width), BF16)],
        compiler_params=params(),
        cost_estimate=pl.CostEstimate(
            flops=2 * vocab * width * channels * parts,
            bytes_accessed=2 * parts * channels * (width + vocab),
            transcendentals=0,
        ),
    )(embedding, gain[None], matrix)


def medium_kernel(
    tok_ref, table_ref, taps_ref, filt_ref, skip_ref, fwd_ref, inv_ref, out_ref, peer_ref,
    proj, gate_f, gate_b, query, spec, freq, zh, zl, inbox, send_sem, recv_sem,
):
    peer = 1 - lax.axis_index("tensor")
    barrier = pltpu.get_barrier_semaphore()
    pl.semaphore_signal(barrier, inc=1, device_id={"tensor": peer}, device_id_type=MESH)
    rows = tok_ref.shape[0]
    vocab = table_ref.shape[1]
    channels = table_ref.shape[2]
    length = rows - HALO
    for part in range(3):
        proj[part, 0:8, :] = jnp.zeros((8, channels), F32)
    third = rows // 3
    for i in range(3):
        picked = onehot(tok_ref[i * third : (i + 1) * third, :], vocab)
        for part in range(3):
            proj[part, 8 + i * third : 8 + (i + 1) * third, :] = dot(picked, table_ref[part])

    @pl.loop(0, rows // 32)
    def _(i):
        row = pl.multiple_of(i * 32, 32)
        taps = [[taps_ref[j, pl.ds(part, 1), :] for j in range(3)] for part in range(3)]
        query[pl.ds(row, 32), :] = short_filter(proj, 0, row, 32, taps[0])
        gate = (
            short_filter(proj, 1, row, 32, taps[1]) * short_filter(proj, 2, row, 32, taps[2])
        ).astype(BF16)
        gate_b[pl.ds(row, 32), :] = gate
        gate_f[pl.ds(row, 32), :] = gate.astype(F32)

    filt = filt_ref[...]
    freq[...] = forward_wide(fwd_ref, filt)
    order = lax.broadcasted_iota(jnp.int32, (BLOCK, BLOCK), 0) + lax.broadcasted_iota(
        jnp.int32, (BLOCK, BLOCK), 1
    )
    flip = (order == BLOCK - 1).astype(BF16)
    high, low = split(filt)
    backward = dot(flip, high) + dot(flip, low)
    last = jnp.sum(backward * gate_f[HALO - BLOCK : HALO, :], axis=0, keepdims=True)
    prior = jnp.sum(backward * gate_f[HALO - BLOCK - 1 : HALO - 1, :], axis=0, keepdims=True)
    at = lax.broadcasted_iota(jnp.int32, (LEAD, channels), 0)
    summed = jnp.where(at == LEAD - 1, last, jnp.where(at == LEAD - 2, prior, 0.0))
    edge = slice(HALO - LEAD, HALO)
    out_ref[0:LEAD, :] = jnp.where(
        at >= LEAD - 2, query[edge, :] * (summed + skip_ref[...] * gate_f[edge, :]), 0.0
    ).astype(BF16)

    pl.semaphore_wait(barrier, 1)
    copies = []
    spec[0] = forward_exact(fwd_ref, gate_b[HALO - BLOCK : HALO, :])
    for b in range(length // BLOCK):
        start = HALO + b * BLOCK
        now, old = (b + 1) % 2, b % 2
        spec[now] = forward_exact(fwd_ref, gate_b[start : start + BLOCK, :])
        for half, sign in ((0, 1.0), (1, -1.0)):

            @pl.loop(0, BLOCK // 64)
            def _(i):
                re = pl.ds(pl.multiple_of(half * (BLOCK // 2) + i * 32, 32), 32)
                im = pl.ds(pl.multiple_of(BLOCK + half * (BLOCK // 2) + i * 32, 32), 32)
                u = spec[now, re, :] - sign * spec[old, im, :]
                v = spec[now, im, :] + sign * spec[old, re, :]
                a, c = freq[re, :], freq[im, :]
                zh[re, :], zl[re, :] = split(u * a - v * c)
                zh[im, :], zl[im, :] = split(u * c + v * a)

        here = slice(start, start + BLOCK)
        conv = inverse_wide(inv_ref, zh, zl)
        out_ref[start - HALO + LEAD : start - HALO + LEAD + BLOCK, :] = (
            query[here, :] * (conv + skip_ref[...] * gate_f[here, :])
        ).astype(BF16)
        first = 0 if b == 0 else LEAD + b * BLOCK
        part = pl.ds(first, LEAD + (b + 1) * BLOCK - first)
        copy = pltpu.make_async_remote_copy(
            src_ref=out_ref.at[part],
            dst_ref=inbox.at[part],
            send_sem=send_sem.at[b],
            recv_sem=recv_sem.at[b],
            device_id={"tensor": peer},
            device_id_type=MESH,
        )
        copy.start()
        copies.append(copy)
    for copy in copies:
        copy.wait()
    peer_ref[...] = inbox[...]


def medium_mix(tokens, table, taps, filt, skip, fwd, inv):
    rows = tokens.shape[0]
    channels = table.shape[2]
    return pl.pallas_call(
        medium_kernel,
        out_shape=[jax.ShapeDtypeStruct((rows - HALO + LEAD, channels), BF16)] * 2,
        scratch_shapes=[
            pltpu.VMEM((3, rows + 8, channels), F32),
            pltpu.VMEM((rows, channels), F32),
            pltpu.VMEM((rows, channels), BF16),
            pltpu.VMEM((rows, channels), F32),
            pltpu.VMEM((2, 2 * BLOCK, channels), F32),
            pltpu.VMEM((2 * BLOCK, channels), F32),
            pltpu.VMEM((2 * BLOCK, channels), BF16),
            pltpu.VMEM((2 * BLOCK, channels), BF16),
            pltpu.VMEM((rows - HALO + LEAD, channels), BF16),
            pltpu.SemaphoreType.DMA(((rows - HALO) // BLOCK,)),
            pltpu.SemaphoreType.DMA(((rows - HALO) // BLOCK,)),
        ],
        compiler_params=params(0),
    )(tokens, table, taps, filt, skip[None], fwd, inv)


def second_kernel(
    size, tok_ref, emb_ref, mix_ref, peer_ref, own_w, peer_w, gain_ref, mat_ref, taps_ref, rate_ref,
    res_ref, skip_ref, fwd_ref, inv_ref, second_ref, mixture_ref,
    acc, normed, proj, gate_f, weight, weight_sem, gate_ref, before_ref, closing_ref,
    segments, enter, gain, kernel, freq, spec, zh, zl, send_sem, recv_sem,
):
    me = lax.axis_index("context")
    barrier = pltpu.get_barrier_semaphore()
    copies = [
        pltpu.make_async_remote_copy(
            src_ref=closing_ref,
            dst_ref=segments.at[me],
            send_sem=send_sem.at[hop],
            recv_sem=recv_sem.at[hop],
            device_id={"context": lax.rem(me + hop, size)},
            device_id_type=MESH,
        )
        for hop in range(1, size)
    ]
    step = pl.program_id(0)
    rows, width = acc.shape
    vocab = emb_ref.shape[0]
    length = rows - LEAD
    channels = mat_ref.shape[1]
    fetch = pltpu.make_async_copy(peer_w, weight, weight_sem)

    @pl.when(step == 0)
    def _():
        fetch.start()
        for hop in range(1, size):
            pl.semaphore_signal(
                barrier, inc=1, device_id={"context": lax.rem(me + hop, size)}, device_id_type=MESH
            )
        picked = onehot(tok_ref[HALO - LEAD :, :], vocab)
        for cols in chunks(width, 384):
            acc[:, cols] = dot(picked, emb_ref[:, cols]) + dot(mix_ref[...], own_w[:, cols])

    @pl.when(step == 1)
    def _():
        fetch.wait()
        for cols in chunks(width, 384):
            acc[:, cols] = acc[:, cols] + dot(peer_ref[...], weight[:, cols])

        @pl.loop(0, rows // 16)
        def _(i):
            at = pl.ds(pl.multiple_of(i * 16, 16), 16)
            row = acc[at, :].astype(BF16)
            second_ref[at, :] = row
            normed[at, :] = normalize(row, gain_ref[...])

    for stage, part in ((1, 1), (2, 2), (3, 0)):

        @pl.when(step == stage)
        def _():
            for cols in chunks(channels):
                proj[part, :, cols] = (
                    dot_nt(normed[...], mat_ref[0, cols, :]).astype(BF16).astype(F32)
                )

    @pl.when(step == 2)
    def _():
        taps = [[taps_ref[j, pl.ds(part, 1), :] for j in range(3)] for part in range(3)]

        @pl.loop(0, length // 32)
        def _(i):
            row = pl.multiple_of(i * 32, 32)
            at = pl.multiple_of(row + LEAD - 8, 8)
            gate = (
                short_filter(proj, 1, at, 32, taps[1]) * short_filter(proj, 2, at, 32, taps[2])
            ).astype(BF16)
            gate_ref[pl.ds(row, 32), :] = gate
            gate_f[pl.ds(row, 32), :] = gate.astype(F32)

        decay = jnp.exp(-rate_ref[...])
        state = jnp.zeros(decay.shape, F32)
        for b in range(length // BLOCK):
            before_ref[b] = state

            def advance(i, state):
                tile8 = gate_f[pl.ds(pl.multiple_of(b * BLOCK + i * 8, 8), 8), :]
                for r in range(8):
                    state = state * decay + tile8[r : r + 1, :]
                return state

            state = lax.fori_loop(0, BLOCK // 8, advance, state)
        closing_ref[...] = state.astype(BF16)
        segments[me] = closing_ref[...]
        pl.semaphore_wait(barrier, size - 1)
        for copy in copies:
            copy.start()

    @pl.when(step == 3)
    def _():
        taps = [taps_ref[j, pl.ds(0, 1), :] for j in range(3)]

        @pl.loop(0, length // 32)
        def _(i):
            row = pl.multiple_of(i * 32, 32)
            at = pl.multiple_of(row + LEAD - 8, 8)
            proj[1, pl.ds(row, 32), :] = short_filter(proj, 0, at, 32, taps)

        rate = rate_ref[...]
        doubled = 2.0 * rate
        series = doubled * (
            1.0
            - doubled * (0.5 - doubled * (1.0 / 6.0 - doubled * (1.0 / 24.0 - doubled / 120.0)))
        )
        gain[...] = res_ref[...] * jnp.sqrt(
            jnp.where(doubled < 0.03, series, 1.0 - jnp.exp(-doubled))
        )
        for lane, span in lanes(channels):

            def store(group, rows):
                kernel[pl.ds(pl.multiple_of(group * 8, 8), 8), lane : lane + span] = rows

            modal_rows(rate_ref, gain, BLOCK // 8, lane, span, store)
        freq[...] = forward_wide(fwd_ref, kernel[...])
        for b in range(length // BLOCK):
            here = slice(b * BLOCK, (b + 1) * BLOCK)
            spec[...] = forward_exact(fwd_ref, gate_ref[here, :])

            @pl.loop(0, BLOCK // 32)
            def _(i):
                re = pl.ds(pl.multiple_of(i * 32, 32), 32)
                im = pl.ds(pl.multiple_of(BLOCK + i * 32, 32), 32)
                u, v = spec[re, :], spec[im, :]
                a, c = freq[re, :], freq[im, :]
                zh[re, :], zl[re, :] = split(u * a - v * c)
                zh[im, :], zl[im, :] = split(u * c + v * a)

            acc[here, :channels] = inverse_wide(inv_ref, zh, zl) + skip_ref[...] * gate_ref[
                here, :
            ].astype(F32)

        for copy in copies:
            copy.wait()
        shard_step = jnp.exp(-rate * float(length))
        incoming = jnp.zeros(rate.shape, F32)
        for source in range(size):
            incoming = jnp.where(
                source < me, incoming * shard_step + segments[source].astype(F32), incoming
            )
        for b in range(length // BLOCK):
            enter[b] = (
                gain[...]
                * jnp.exp(-rate)
                * (before_ref[b] + jnp.exp(-rate * float(b * BLOCK)) * incoming)
            )
        for b in range(length // BLOCK):
            for lane, span in lanes(channels):
                cols = slice(lane, lane + span)

                def store(group, rows):
                    at = pl.ds(pl.multiple_of(b * BLOCK + group * 8, 8), 8)
                    acc[at, cols] = proj[1, at, cols] * (acc[at, cols] + rows)

                modal_rows(rate_ref, enter.at[b], BLOCK // 8, lane, span, store)
            here = slice(b * BLOCK, (b + 1) * BLOCK)
            mixture_ref[here, :] = acc[here, :channels].astype(BF16)


def second_block(size, residue, skip, fwd, inv, tokens, embedding, mix, peer_mix, weights, peer_weights, gain, matrix, taps, rate):
    rows, channels = mix.shape
    vocab, width = embedding.shape
    length = rows - LEAD
    modes = rate.shape[0]
    whole2 = lambda i: (0, 0)
    whole3 = lambda i: (0, 0, 0)
    once = dict(pipeline_mode=pl.Buffered(1))
    return pl.pallas_call(
        functools.partial(second_kernel, size),
        grid=(4,),
        in_specs=[
            pl.BlockSpec(tokens.shape, whole2),
            pl.BlockSpec((vocab, width), whole2, **once),
            pl.BlockSpec((rows, channels), whole2, **once),
            pl.BlockSpec((rows, channels), whole2, **once),
            pl.BlockSpec((channels, width), whole2, **once),
            pl.BlockSpec(memory_space=pl.ANY),
            pl.BlockSpec((1, width), whole2),
            pl.BlockSpec(
                (1, channels, width),
                lambda i: (jnp.where(i == 3, 0, jnp.where(i == 2, 2, 1)), 0, 0),
            ),
            pl.BlockSpec(taps.shape, whole3),
            pl.BlockSpec(rate.shape, whole2),
            pl.BlockSpec(rate.shape, whole2),
            pl.BlockSpec((1, channels), whole2),
            pl.BlockSpec(fwd.shape, whole2),
            pl.BlockSpec(inv.shape, whole2),
        ],
        out_specs=[
            pl.BlockSpec((rows, width), whole2),
            pl.BlockSpec((length, channels), whole2),
        ],
        out_shape=[
            jax.ShapeDtypeStruct((rows, width), BF16),
            jax.ShapeDtypeStruct((length, channels), BF16),
        ],
        scratch_shapes=[
            pltpu.VMEM((rows, width), F32),
            pltpu.VMEM((rows, width), BF16),
            pltpu.VMEM((3, rows, channels), F32),
            pltpu.VMEM((length, channels), F32),
            pltpu.VMEM((channels, width), BF16),
            pltpu.SemaphoreType.DMA,
            pltpu.VMEM((length, channels), BF16),
            pltpu.VMEM((length // BLOCK, modes, channels), F32),
            pltpu.VMEM((modes, channels), BF16),
            pltpu.VMEM((size, modes, channels), BF16),
            pltpu.VMEM((length // BLOCK, modes, channels), F32),
            pltpu.VMEM((modes, channels), F32),
            pltpu.VMEM((BLOCK, channels), F32),
            pltpu.VMEM((2 * BLOCK, channels), F32),
            pltpu.VMEM((2 * BLOCK, channels), F32),
            pltpu.VMEM((2 * BLOCK, channels), BF16),
            pltpu.VMEM((2 * BLOCK, channels), BF16),
            pltpu.SemaphoreType.DMA((size,)),
            pltpu.SemaphoreType.DMA((size,)),
        ],
        compiler_params=params(1),
    )(
        tokens, embedding, mix, peer_mix, weights, peer_weights, gain[None], matrix, taps, rate,
        residue, skip[None], fwd, inv,
    )


def lanes(channels):
    return [(at, min(128, channels - at)) for at in range(0, channels, 128)]


def modal_rows(rate_ref, coef_ref, groups, lane, width, store):
    modes = rate_ref.shape[0]
    at = lax.broadcasted_iota(jnp.int32, (8, width), 0).astype(F32)
    cols = slice(lane, lane + width)
    values, steps = [], []
    for m in range(modes):
        rate = rate_ref[m : m + 1, cols]
        values.append(coef_ref[m : m + 1, cols] * jnp.exp(-rate * at))
        steps.append(jnp.broadcast_to(jnp.exp(-8.0 * rate), (8, width)))

    def advance(group, values):
        terms = list(values)
        while len(terms) > 1:
            terms = [a + b for a, b in zip(terms[::2], terms[1::2])] + (
                [terms[-1]] if len(terms) % 2 else []
            )
        store(group, terms[0])
        return [v * s for v, s in zip(values, steps)]

    lax.fori_loop(0, groups, advance, values)


def on_device(
    tokens, embedding, gain_a, in_proj_a, short_a, mr_filter, mr_skip, out_proj_a,
    gain_b, in_proj_b, short_b, li_rate, li_residue, li_skip, out_proj_b,
):
    fwd, inv = [jnp.asarray(m) for m in transforms()]
    own_rows = tokens.shape[0]
    length = own_rows * lax.axis_size("tensor")
    position = lax.axis_index("context")
    side = lax.axis_index("tensor")
    swap = [(0, 1), (1, 0)]
    size = lax.axis_size("context")
    both = ("context", "tensor")
    other_tokens = lax.ppermute(tokens, "tensor", swap)
    edge = tokens[own_rows - HALO :]
    halo = sum(
        lax.ppermute(edge, both, [(2 * c + 1, 2 * c + 2 + t) for c in range(size - 1)])
        for t in range(2)
    )
    weights_a = lax.ppermute(out_proj_a, "tensor", swap)
    weights_b = lax.ppermute(out_proj_b, "tensor", swap)
    table = make_table(embedding, gain_a, in_proj_a)
    near = jnp.concatenate(
        [
            jnp.where(position == 0, -1, halo),
            jnp.where(side == 0, tokens, other_tokens),
            jnp.where(side == 0, other_tokens, tokens),
        ]
    )
    mixed, peer_mixed = medium_mix(near[:, None], table, short_a, mr_filter, mr_skip, fwd, inv)
    second, mixture = second_block(
        size, li_residue, li_skip, fwd, inv, near[:, None], embedding, mixed, peer_mixed,
        out_proj_a, weights_a, gain_b, in_proj_b, short_b, li_rate,
    )
    sent = lax.dynamic_slice_in_dim(mixture, (1 - side) * own_rows, own_rows, 0)
    kept = lax.dynamic_slice_in_dim(mixture, side * own_rows, own_rows, 0)
    other = lax.ppermute(sent, "tensor", swap)
    residual = lax.dynamic_slice_in_dim(second, LEAD + side * own_rows, own_rows, 0)
    summed = residual.astype(F32) + dot(kept, out_proj_b)
    return (summed + dot(other, weights_b)).astype(BF16)


def solution(mesh):
    return jax.shard_map(
        on_device,
        mesh=mesh,
        in_specs=(
            P(("context", "tensor")),
            P(),
            P(),
            P(None, "tensor", None),
            P(None, None, "tensor"),
            P(None, "tensor"),
            P("tensor"),
            P("tensor", None),
            P(),
            P(None, "tensor", None),
            P(None, None, "tensor"),
            P(None, "tensor"),
            P(None, "tensor"),
            P("tensor"),
            P("tensor", None),
        ),
        out_specs=P(("context", "tensor"), None),
        check_vma=False,
    )
```
